32 devices in a mesh: ctx: 2 (over x), kvh: 4 (over z), rep: 4 (over y, core).
Axes of the slice: x: 2, y: 2, z: 4, core: 2. Of those that a mesh axis runs over, the one named last changes fastest.
Arguments:
- query: bfloat16 [256, 16384], P(('rep', 'ctx'), 'kvh'), parts along dimension 0, may hold values from -160 to 160
- slab_keys: bfloat16 [256, 1024], P(('rep', 'ctx'), 'kvh'), parts along dimension 0, may hold values from -6 to 6
- slab_values: bfloat16 [256, 1024], P(('rep', 'ctx'), 'kvh'), parts along dimension 0, may hold values from -6 to 6
- ctx_keys: bfloat16 [16384, 1024], P(('rep', 'ctx'), 'kvh'), parts along dimension 0, may hold values from -7 to 7
- ctx_values: bfloat16 [16384, 1024], P(('rep', 'ctx'), 'kvh'), parts along dimension 0, may hold values from -6 to 6
- prompt_len: int32 [16], P('rep'), parts along dimension 0, may hold values from 2049 to 4096, as said below
- cont_len: int32 [16], P('rep'), parts along dimension 0, may hold values from 1 to 24, 64 in all
- slab_order: int32 [16], P('rep'), parts along dimension 0, may hold values from 0 to 3, as said below
Outputs:
- attention: bfloat16 [256, 16384], P(('rep', 'ctx'), 'kvh'), parts along dimension 0
The draws below stay inside these ranges and needn't reach their ends.
There are 4 independent parts, one for each index of `rep`. The reference program is written for one: setup_inputs(seed, part) draws one part's arguments, and reference() takes and returns one part's arrays. A program takes and returns all parts, laid end to end along the dimension named above; each array names one. Nothing has to cross between parts.
Inputs may be any that keep to these rules, and one draw needn't show every extreme that they name: `prompt_len`: 4 prompt lengths, the largest exactly 4096. `cont_len`: 4 continuation lengths summing to 64, the largest exactly 24. `slab_order`: each span of 0 to 3 once.
All inputs are finite; a program needn't handle non-finite values.
Results may differ from the reference program's by a relative error of at most 0.0044.
Values may be sent and summed in bfloat16 or wider, within the bound.
A program may use at most 128 MiB of HBM per device.

```python
import math
import jax
import jax.numpy as jnp
import numpy as np
from jax import lax

HEADS = 128
KV_HEADS = 8
HEAD_DIM = 128
SC = 16
ROLLOUTS = 4
SPANS = 4
QS = 64
CTX = 4096
CMOST = 24


def context_base(key):
    base_key = jax.random.fold_in(key, 101)
    return jnp.clip(jax.random.normal(base_key, (CTX, KV_HEADS * HEAD_DIM), jnp.float32), -6.0, 6.0)


def draw_ctx_keys(key, part):
    base = context_base(key)
    return base.astype(jnp.bfloat16)


def draw_query(key, part):
    own_key = jax.random.fold_in(key, 3)
    return jnp.clip(2.5 * jax.random.normal(own_key, (QS, HEADS * HEAD_DIM), jnp.float32), -15.0, 15.0).astype(jnp.bfloat16)


def draw_prompt_len(key, part):
    key = jax.random.fold_in(key, 11)
    lengths = jax.random.randint(jax.random.fold_in(key, 1), (ROLLOUTS,), CTX // 2 + 1, CTX + 1)
    chosen = jax.random.randint(jax.random.fold_in(key, 2), (), 0, ROLLOUTS)
    slots = jnp.arange(ROLLOUTS, dtype=jnp.int32)
    return jnp.where(slots == chosen, CTX, lengths).astype(jnp.int32)


def draw_slab_order(key, part):
    key = jax.random.fold_in(key, 13)
    return jax.random.permutation(key, jnp.arange(SPANS, dtype=jnp.int32)).astype(jnp.int32)


def levels(rng, shape, pieces, smallest, largest):
    gain, own = 1.0, jax.random.fold_in(rng, 6)
    for axis_at, shards_of in pieces:
        draws = jnp.exp(jax.random.uniform(jax.random.fold_in(own, axis_at), (shards_of,), jnp.float32, smallest / len(pieces), largest / len(pieces)))
        gain = gain * jnp.repeat(draws, shape[axis_at] // shards_of).reshape([-1 if axis == axis_at else 1 for axis in range(len(shape))])
    return gain


def split_up(amount, total, reach, lean):
    loads = [(1 << 20) // math.isqrt(grade ** lean) + 1 for grade in range(2, amount + 1)]
    surplus, given = total - reach - (amount - 1), [1] * (amount - 1)
    while surplus > 0:
        free = [i for i in range(amount - 1) if given[i] < reach]
        mass, left = sum([loads[i] for i in free]), surplus
        for i in free:
            addition = min(reach - given[i], max(1, left * loads[i] // mass), surplus)
            given[i] = given[i] + addition
            surplus = surplus - addition
    return np.array([reach] + given)


def uneven(stream_key, number_of, total, most, skew):
    if number_of == 2:
        one = jax.random.randint(stream_key, (), max(1, total - most), min(most, total - 1) + 1)
        return jnp.stack([one, total - one])
    sizes = jnp.asarray(split_up(number_of, total, most, skew), jnp.int32)
    couples = (number_of - 1) // 2
    giver, receiver = sizes[1:1 + 2 * couples:2], sizes[2:2 + 2 * couples:2]
    room = jnp.minimum(giver - 1, most - receiver)
    moved = jax.random.randint(jax.random.fold_in(stream_key, 1), (couples,), 0, 1 << 20) % (room + 1)
    sizes = sizes.at[1:1 + 2 * couples:2].set(giver - moved).at[2:2 + 2 * couples:2].set(receiver + moved)
    return sizes[jax.random.permutation(jax.random.fold_in(stream_key, 2), number_of)]


def bell_draw(key, dims, width, limit, pieces=(), kind=jnp.bfloat16):
    gain = levels(key, dims, pieces, -0.22, 0.18) if pieces else 1.0
    entries = jax.random.normal(key, dims, jnp.float32) * width * gain
    return jnp.minimum(jnp.maximum(entries, -limit), limit).astype(kind)


def setup_inputs(seed: int = 0, part: int = 0) -> dict:
    key_of = jax.random.split(jax.random.key(seed), 9)
    part_splits = jax.random.split(jax.random.fold_in(key_of[8], part), 9)
    return {
        "query": draw_query(jax.random.fold_in(jax.random.fold_in(key_of[8], part), 71), part),
        "slab_keys": bell_draw(part_splits[1], (QS, KV_HEADS * HEAD_DIM), 1.0, 6.0, ((0, 2), (1, 4))),
        "slab_values": bell_draw(part_splits[2], (QS, KV_HEADS * HEAD_DIM), 1.0, 6.0, ((0, 2), (1, 4))),
        "ctx_keys": draw_ctx_keys(jax.random.fold_in(jax.random.fold_in(key_of[8], part), 71), part),
        "ctx_values": bell_draw(part_splits[4], (CTX, KV_HEADS * HEAD_DIM), 1.0, 6.0, ((0, 2), (1, 4))),
        "prompt_len": draw_prompt_len(jax.random.fold_in(jax.random.fold_in(key_of[8], part), 71), part),
        "cont_len": uneven(part_splits[6], ROLLOUTS, QS, CMOST, 2).astype(jnp.int32),
        "slab_order": draw_slab_order(jax.random.fold_in(jax.random.fold_in(key_of[8], part), 71), part),
    }


def rollout_of(positions, ends):
    return jnp.sum((positions[:, None] >= ends[None, :]).astype(jnp.int32), axis=1)


def reference(query, slab_keys, slab_values, ctx_keys, ctx_values, prompt_len, cont_len, slab_order):
    row_ids = jnp.arange(QS, dtype=jnp.int32)
    places = (slab_order[row_ids // SC] * SC + row_ids % SC).astype(jnp.int32)
    cont_end = jnp.cumsum(cont_len).astype(jnp.int32)
    query_roll = rollout_of(places, cont_end)
    query_limit = prompt_len[query_roll].astype(jnp.int32)
    key_roll = jnp.concatenate([jnp.full((CTX,), -1, jnp.int32), query_roll])
    key_place = jnp.concatenate([jnp.arange(CTX, dtype=jnp.int32), places])
    total_keys = CTX + QS
    key_heads = jnp.concatenate([ctx_keys, slab_keys]).reshape(total_keys, KV_HEADS, HEAD_DIM).transpose(1, 0, 2)
    value_heads = jnp.concatenate([ctx_values, slab_values]).reshape(total_keys, KV_HEADS, HEAD_DIM).transpose(1, 0, 2)
    group = HEADS // KV_HEADS
    block_rows = math.gcd(QS, 128)
    blocks = QS // block_rows
    query_blocks = query.reshape(blocks, block_rows, KV_HEADS, group, HEAD_DIM)
    score_scale = HEAD_DIM ** -0.5

    def per_block(operands):
        query_block, roll_block, place_block, limit_block = operands
        in_context = key_roll[None, :] < 0
        same_roll = (key_roll[None, :] == roll_block[:, None]) & (key_place[None, :] <= place_block[:, None])
        visible = jnp.where(in_context, key_place[None, :] < limit_block[:, None], same_roll)

        def per_group(group_operands):
            query_group, key_group, value_group = group_operands
            scores = jnp.einsum("qhd,kd->hqk", query_group.astype(jnp.float32), key_group.astype(jnp.float32)) * score_scale
            scores = jnp.where(visible[None, :, :], scores, -jnp.inf)
            top = jnp.max(scores, axis=-1)
            weights = jnp.exp(scores - top[..., None])
            total = jnp.sum(weights, axis=-1)
            rounded = lax.optimization_barrier(weights.astype(jnp.bfloat16)).astype(jnp.float32)
            numerator = jnp.einsum("hqk,kd->qhd", rounded, value_group.astype(jnp.float32))
            return numerator / total.T[..., None]

        outs = lax.map(per_group, (query_block.transpose(1, 0, 2, 3), key_heads, value_heads))
        return outs.transpose(1, 0, 2, 3).reshape(block_rows, HEADS * HEAD_DIM).astype(jnp.bfloat16)

    result = lax.map(per_block, (query_blocks, query_roll.reshape(blocks, block_rows), places.reshape(blocks, block_rows), query_limit.reshape(blocks, block_rows)))
    return result.reshape(QS, HEADS * HEAD_DIM)
```

```python
import jax
import jax.numpy as jnp
from jax import lax
from jax.experimental import pallas as pl
from jax.experimental.pallas import tpu as pltpu
from jax.sharding import PartitionSpec as P

HEADS = 128
KV_HEADS = 8
HEAD_DIM = 128
GROUP = HEADS // KV_HEADS
LOG2E = 1.4426950408889634
SCALE2 = HEAD_DIM ** -0.5 * LOG2E
LOWEST = -1e30
MESH = pl.DeviceIdType.MESH

CHUNK_HEADS = 8
LEAD = 2


def make_kernel(n, rows, cols, keys, spans):
    groups = cols // (GROUP * HEAD_DIM)
    width = CHUNK_HEADS * HEAD_DIM
    chunks = cols // width
    per_group = chunks // groups
    span = rows * n // spans
    local_spans = rows // span
    total_items = n * chunks
    own = n - 1
    lead = LEAD

    def kernel(prompt_ref, cont_ref, order_ref, q_hbm, sk_hbm, sv_hbm, ck_hbm, cv_hbm, out_ref,
               qbuf, kbuf, vbuf, skbuf, svbuf, osend, orecv, oown, lse, lrecv,
               local_sem, q_send, q_recv, o_send, o_recv, l_send, l_recv):
        me = lax.axis_index("ctx")

        local_copies = []
        for g in range(groups):
            lanes = slice(g * HEAD_DIM, (g + 1) * HEAD_DIM)
            for i, (src, dst) in enumerate((
                (ck_hbm.at[:, lanes], kbuf.at[g]),
                (cv_hbm.at[:, lanes], vbuf.at[g]),
                (sk_hbm.at[:, lanes], skbuf.at[g, 0:rows]),
                (sv_hbm.at[:, lanes], svbuf.at[g, 0:rows]),
            )):
                local_copies.append(pltpu.make_async_copy(src, dst, local_sem.at[g * 4 + i]))
        local_copies.append(pltpu.make_async_copy(q_hbm, qbuf.at[own], local_sem.at[groups * 4]))
        for copy in local_copies:
            copy.start()

        barrier = pltpu.get_barrier_semaphore()
        for d in range(1, n):
            pl.semaphore_signal(barrier, inc=1, device_id={"ctx": lax.rem(me + d, n)}, device_id_type=MESH)

        pad = skbuf.shape[1] - rows
        for g in range(groups):
            skbuf[g, rows:, :] = jnp.zeros((pad, HEAD_DIM), jnp.bfloat16)
            svbuf[g, rows:, :] = jnp.zeros((pad, HEAD_DIM), jnp.bfloat16)

        pl.semaphore_wait(barrier, n - 1)

        def q_copy(slot, c):
            at = pl.ds(pl.multiple_of(c * width, width), width)
            return pltpu.make_async_remote_copy(
                src_ref=q_hbm.at[:, at], dst_ref=qbuf.at[slot, :, at],
                send_sem=q_send.at[slot, c], recv_sem=q_recv.at[slot, c],
                device_id={"ctx": lax.rem(me + slot + 1, n)}, device_id_type=MESH)

        def o_copy(slot, c):
            at = pl.ds(pl.multiple_of(c * width, width), width)
            return pltpu.make_async_remote_copy(
                src_ref=osend.at[slot, :, at], dst_ref=orecv.at[slot, :, at],
                send_sem=o_send.at[slot, c], recv_sem=o_recv.at[slot, c],
                device_id={"ctx": lax.rem(me + 2 * n - slot - 1, n)}, device_id_type=MESH)

        def l_copy(slot):
            return pltpu.make_async_remote_copy(
                src_ref=lse.at[slot], dst_ref=lrecv.at[slot],
                send_sem=l_send.at[slot], recv_sem=l_recv.at[slot],
                device_id={"ctx": lax.rem(me + 2 * n - slot - 1, n)}, device_id_type=MESH)

        for slot in range(n - 1):
            for c in range(chunks):
                q_copy(slot, c).start()
        for copy in local_copies:
            copy.wait()

        ends, prompts, at_end = [], [], 0
        for r in range(prompt_ref.shape[0]):
            at_end = at_end + cont_ref[r]
            ends.append(at_end)
            prompts.append(prompt_ref[r])

        def facts(shape, dim, device):
            ids = lax.broadcasted_iota(jnp.int32, shape, dim)
            place = ids
            for k in range(local_spans):
                start = order_ref[device * local_spans + k] * span - k * span
                inside = (ids >= k * span) & (ids < (k + 1) * span)
                place = jnp.where(inside, ids + start, place)
            roll = jnp.zeros(shape, jnp.int32)
            for end in ends:
                roll = roll + (place >= end).astype(jnp.int32)
            return place, roll

        key_place, key_roll = facts((rows, skbuf.shape[1]), 1, me)
        key_is = lax.broadcasted_iota(jnp.int32, (rows, skbuf.shape[1]), 1) < rows
        lane = lax.broadcasted_iota(jnp.int32, (rows, 128), 1)

        def step(t, carry):
            item = lax.rem(t + total_items - lead, total_items)
            slot = item // chunks
            c = lax.rem(item, chunks)
            g = c // per_group
            source = lax.rem(me + 2 * n - slot - 1, n)

            @pl.when(slot < own)
            def _():
                q_copy(slot, c).wait_recv()

            row_place, row_roll = facts((rows, 128), 0, source)
            limit = jnp.zeros((rows, 128), jnp.int32)
            for r, prompt in enumerate(prompts):
                limit = jnp.where(row_roll == r, prompt, limit)
            limit = limit[:, :1] - me * keys
            slab_bias = jnp.where(
                key_is & (key_roll == row_roll) & (key_place <= row_place), 0.0, LOWEST)

            at = pl.ds(pl.multiple_of(c * width, width), width)
            q = qbuf[slot, :, at]
            q = jnp.concatenate(
                [q[:, h * HEAD_DIM:(h + 1) * HEAD_DIM] for h in range(CHUNK_HEADS)], axis=0)
            dims = (((1,), (1,)), ((), ()))
            s_ctx = lax.dot_general(q, kbuf[g], dims, preferred_element_type=jnp.float32)
            s_slab = lax.dot_general(q, skbuf[g], dims, preferred_element_type=jnp.float32)
            limits = jnp.concatenate([limit] * CHUNK_HEADS, axis=0)
            columns = lax.broadcasted_iota(jnp.int32, s_ctx.shape, 1)
            s_ctx = jnp.where(columns < limits, s_ctx, LOWEST)
            s_slab = s_slab + jnp.concatenate([slab_bias] * CHUNK_HEADS, axis=0)
            top = jnp.maximum(
                jnp.max(s_ctx, axis=1, keepdims=True), jnp.max(s_slab, axis=1, keepdims=True))
            p_ctx = jnp.exp2((s_ctx - top) * SCALE2)
            p_slab = jnp.exp2((s_slab - top) * SCALE2)
            total = jnp.sum(p_ctx, axis=1, keepdims=True) + jnp.sum(p_slab, axis=1, keepdims=True)
            o = jnp.dot(p_ctx.astype(jnp.bfloat16), vbuf[g], preferred_element_type=jnp.float32)
            o = o + jnp.dot(p_slab.astype(jnp.bfloat16), svbuf[g], preferred_element_type=jnp.float32)
            o = o * (1.0 / total)
            level = top * SCALE2 + jnp.log2(total)
            levels = lse[slot]
            for h in range(CHUNK_HEADS):
                levels = jnp.where(
                    lane == c * CHUNK_HEADS + h, level[h * rows:(h + 1) * rows], levels)
            lse[slot] = levels
            o = jnp.concatenate(
                [o[h * rows:(h + 1) * rows] for h in range(CHUNK_HEADS)], axis=1)

            @pl.when(slot == own)
            def _():
                oown[:, at] = o

            @pl.when(slot < own)
            def _():
                osend[slot, :, at] = o.astype(jnp.bfloat16)
                o_copy(slot, c).start()

                @pl.when(c == chunks - 1)
                def _():
                    l_copy(slot).start()

            return carry

        for slot in range(n):
            lse[slot] = jnp.zeros((rows, 128), jnp.float32)
        lax.fori_loop(0, total_items, step, 0)

        for slot in range(n - 1):
            for c in range(chunks):
                o_copy(slot, c).wait_recv()
            l_copy(slot).wait_recv()
        levels = [lrecv[slot] for slot in range(n - 1)] + [lse[own]]
        top = levels[0]
        for level in levels[1:]:
            top = jnp.maximum(top, level)
        shares = [jnp.exp2(level - top) for level in levels]
        whole = shares[0]
        for share in shares[1:]:
            whole = whole + share
        shares = [share / whole for share in shares]
        for h in range(cols // HEAD_DIM):
            at = slice(h * HEAD_DIM, (h + 1) * HEAD_DIM)
            mixed = oown[:, at] * shares[own][:, h:h + 1]
            for slot in range(n - 1):
                mixed = mixed + orecv[slot, :, at].astype(jnp.float32) * shares[slot][:, h:h + 1]
            out_ref[:, at] = mixed.astype(jnp.bfloat16)
        for slot in range(n - 1):
            for c in range(chunks):
                q_copy(slot, c).wait_send()
                o_copy(slot, c).wait_send()
            l_copy(slot).wait_send()

    return kernel, chunks, groups


def solution(mesh):
    n = mesh.shape["ctx"]

    def local(query, slab_keys, slab_values, ctx_keys, ctx_values, prompt_len, cont_len, slab_order):
        rows, cols = query.shape
        keys = ctx_keys.shape[0]
        kernel, chunks, groups = make_kernel(n, rows, cols, keys, slab_order.shape[0])
        slab_pad = -(-rows // 128) * 128
        smem = pl.BlockSpec(memory_space=pltpu.SMEM)
        anywhere = pl.BlockSpec(memory_space=pl.ANY)
        bf16, f32 = jnp.bfloat16, jnp.float32
        dma = pltpu.SemaphoreType.DMA
        return pl.pallas_call(
            kernel,
            out_shape=jax.ShapeDtypeStruct((rows, cols), bf16),
            in_specs=[smem] * 3 + [anywhere] * 5,
            out_specs=pl.BlockSpec(memory_space=pltpu.VMEM),
            scratch_shapes=[
                pltpu.VMEM((n, rows, cols), bf16),
                pltpu.VMEM((groups, keys, HEAD_DIM), bf16),
                pltpu.VMEM((groups, keys, HEAD_DIM), bf16),
                pltpu.VMEM((groups, slab_pad, HEAD_DIM), bf16),
                pltpu.VMEM((groups, slab_pad, HEAD_DIM), bf16),
                pltpu.VMEM((n - 1, rows, cols), bf16),
                pltpu.VMEM((n - 1, rows, cols), bf16),
                pltpu.VMEM((rows, cols), f32),
                pltpu.VMEM((n, rows, 128), f32),
                pltpu.VMEM((n - 1, rows, 128), f32),
                dma((4 * groups + 1,)),
                dma((n - 1, chunks)),
                dma((n - 1, chunks)),
                dma((n - 1, chunks)),
                dma((n - 1, chunks)),
                dma((n - 1,)),
                dma((n - 1,)),
            ],
            compiler_params=pltpu.CompilerParams(
                collective_id=0, has_side_effects=True, vmem_limit_bytes=56 * 1024 * 1024),
        )(prompt_len, cont_len, slab_order, query, slab_keys, slab_values, ctx_keys, ctx_values)

    placed = (P(("rep", "ctx"), "kvh"),) * 5 + (P("rep"),) * 3
    return jax.shard_map(
        local, mesh=mesh, in_specs=placed, out_specs=P(("rep", "ctx"), "kvh"), check_vma=False)
```

```python
import jax
import jax.numpy as jnp
from jax import lax
from jax.experimental import pallas as pl
from jax.experimental.pallas import tpu as pltpu
from jax.sharding import PartitionSpec as P

HEADS = 128
KV_HEADS = 8
HEAD_DIM = 128
GROUP = HEADS // KV_HEADS
LOG2E = 1.4426950408889634
SCALE2 = HEAD_DIM ** -0.5 * LOG2E
LOWEST = -1e30
MESH = pl.DeviceIdType.MESH

CHUNK_HEADS = 8
LEAD = 2


def make_kernel(n, rows, cols, keys, spans):
    groups = cols // (GROUP * HEAD_DIM)
    width = CHUNK_HEADS * HEAD_DIM
    chunks = cols // width
    per_group = chunks // groups
    span = rows * n // spans
    local_spans = rows // span
    total_items = n * chunks
    own = n - 1
    lead = LEAD

    def kernel(prompt_hbm, cont_hbm, order_hbm, q_hbm, sk_hbm, sv_hbm, ck_hbm, cv_hbm, out_ref,
               prompt_ref, cont_ref, order_ref, qbuf, kbuf, vbuf, skbuf, svbuf, osend, orecv, oown, lse, lrecv,
               local_sem, q_send, q_recv, o_send, o_recv, l_send, l_recv):
        me = lax.axis_index("ctx")

        barrier = pltpu.get_barrier_semaphore()
        for d in range(1, n):
            pl.semaphore_signal(barrier, inc=1, device_id={"ctx": lax.rem(me + d, n)}, device_id_type=MESH)

        local_copies = []
        for g in range(groups):
            lanes = slice(g * HEAD_DIM, (g + 1) * HEAD_DIM)
            for i, (src, dst) in enumerate((
                (ck_hbm.at[:, lanes], kbuf.at[g]),
                (cv_hbm.at[:, lanes], vbuf.at[g]),
                (sk_hbm.at[:, lanes], skbuf.at[g, 0:rows]),
                (sv_hbm.at[:, lanes], svbuf.at[g, 0:rows]),
            )):
                local_copies.append(pltpu.make_async_copy(src, dst, local_sem.at[g * 4 + i]))
        local_copies.append(pltpu.make_async_copy(q_hbm, qbuf.at[own], local_sem.at[groups * 4]))
        for i, (src, dst) in enumerate((
            (prompt_hbm, prompt_ref), (cont_hbm, cont_ref), (order_hbm, order_ref))):
            local_copies.append(pltpu.make_async_copy(src, dst, local_sem.at[groups * 4 + 1 + i]))
        for copy in local_copies:
            copy.start()

        pad = skbuf.shape[1] - rows
        for g in range(groups):
            skbuf[g, rows:, :] = jnp.zeros((pad, HEAD_DIM), jnp.bfloat16)
            svbuf[g, rows:, :] = jnp.zeros((pad, HEAD_DIM), jnp.bfloat16)

        pl.semaphore_wait(barrier, n - 1)

        def q_copy(slot, c):
            at = pl.ds(pl.multiple_of(c * width, width), width)
            return pltpu.make_async_remote_copy(
                src_ref=q_hbm.at[:, at], dst_ref=qbuf.at[slot, :, at],
                send_sem=q_send.at[slot, c], recv_sem=q_recv.at[slot, c],
                device_id={"ctx": lax.rem(me + slot + 1, n)}, device_id_type=MESH)

        def o_copy(slot, c):
            at = pl.ds(pl.multiple_of(c * width, width), width)
            return pltpu.make_async_remote_copy(
                src_ref=osend.at[slot, :, at], dst_ref=orecv.at[slot, :, at],
                send_sem=o_send.at[slot, c], recv_sem=o_recv.at[slot, c],
                device_id={"ctx": lax.rem(me + 2 * n - slot - 1, n)}, device_id_type=MESH)

        def l_copy(slot):
            return pltpu.make_async_remote_copy(
                src_ref=lse.at[slot], dst_ref=lrecv.at[slot],
                send_sem=l_send.at[slot], recv_sem=l_recv.at[slot],
                device_id={"ctx": lax.rem(me + 2 * n - slot - 1, n)}, device_id_type=MESH)

        for slot in range(n - 1):
            for c in range(chunks):
                q_copy(slot, c).start()
        for copy in local_copies:
            copy.wait()

        ends, prompts, at_end = [], [], 0
        for r in range(prompt_ref.shape[0]):
            at_end = at_end + cont_ref[r]
            ends.append(at_end)
            prompts.append(prompt_ref[r])

        def facts(shape, dim, device):
            ids = lax.broadcasted_iota(jnp.int32, shape, dim)
            place = ids
            for k in range(local_spans):
                start = order_ref[device * local_spans + k] * span - k * span
                inside = (ids >= k * span) & (ids < (k + 1) * span)
                place = jnp.where(inside, ids + start, place)
            roll = jnp.zeros(shape, jnp.int32)
            for end in ends:
                roll = roll + (place >= end).astype(jnp.int32)
            return place, roll

        key_place, key_roll = facts((rows, skbuf.shape[1]), 1, me)
        key_is = lax.broadcasted_iota(jnp.int32, (rows, skbuf.shape[1]), 1) < rows
        lane = lax.broadcasted_iota(jnp.int32, (rows, 128), 1)

        def step(t, carry):
            item = lax.rem(t + total_items - lead, total_items)
            slot = item // chunks
            c = lax.rem(item, chunks)
            g = c // per_group
            source = lax.rem(me + 2 * n - slot - 1, n)

            @pl.when(slot < own)
            def _():
                q_copy(slot, c).wait_recv()

            row_place, row_roll = facts((rows, 128), 0, source)
            limit = jnp.zeros((rows, 128), jnp.int32)
            for r, prompt in enumerate(prompts):
                limit = jnp.where(row_roll == r, prompt, limit)
            limit = limit[:, :1] - me * keys
            slab_bias = jnp.where(
                key_is & (key_roll == row_roll) & (key_place <= row_place), 0.0, LOWEST)

            at = pl.ds(pl.multiple_of(c * width, width), width)
            q = qbuf[slot, :, at]
            q = jnp.concatenate(
                [q[:, h * HEAD_DIM:(h + 1) * HEAD_DIM] for h in range(CHUNK_HEADS)], axis=0)
            dims = (((1,), (1,)), ((), ()))
            s_ctx = lax.dot_general(q, kbuf[g], dims, preferred_element_type=jnp.float32)
            s_slab = lax.dot_general(q, skbuf[g], dims, preferred_element_type=jnp.float32)
            limits = jnp.concatenate([limit] * CHUNK_HEADS, axis=0)
            columns = lax.broadcasted_iota(jnp.int32, s_ctx.shape, 1)
            s_ctx = jnp.where(columns < limits, s_ctx, LOWEST)
            s_slab = s_slab + jnp.concatenate([slab_bias] * CHUNK_HEADS, axis=0)
            top = jnp.maximum(
                jnp.max(s_ctx, axis=1, keepdims=True), jnp.max(s_slab, axis=1, keepdims=True))
            p_ctx = jnp.exp2((s_ctx - top) * SCALE2)
            p_slab = jnp.exp2((s_slab - top) * SCALE2)
            total = jnp.sum(p_ctx, axis=1, keepdims=True) + jnp.sum(p_slab, axis=1, keepdims=True)
            o = jnp.dot(p_ctx.astype(jnp.bfloat16), vbuf[g], preferred_element_type=jnp.float32)
            o = o + jnp.dot(p_slab.astype(jnp.bfloat16), svbuf[g], preferred_element_type=jnp.float32)
            o = o * (1.0 / total)
            level = top * SCALE2 + jnp.log2(total)
            levels = lse[slot]
            for h in range(CHUNK_HEADS):
                levels = jnp.where(
                    lane == c * CHUNK_HEADS + h, level[h * rows:(h + 1) * rows], levels)
            lse[slot] = levels
            o = jnp.concatenate(
                [o[h * rows:(h + 1) * rows] for h in range(CHUNK_HEADS)], axis=1)

            @pl.when(slot == own)
            def _():
                oown[:, at] = o

            @pl.when(slot < own)
            def _():
                osend[slot, :, at] = o.astype(jnp.bfloat16)
                o_copy(slot, c).start()

                @pl.when(c == chunks - 1)
                def _():
                    l_copy(slot).start()

            return carry

        for slot in range(n):
            lse[slot] = jnp.zeros((rows, 128), jnp.float32)
        lax.fori_loop(0, total_items, step, 0)

        for slot in range(n - 1):
            for c in range(chunks):
                o_copy(slot, c).wait_recv()
            l_copy(slot).wait_recv()
        levels = [lrecv[slot] for slot in range(n - 1)] + [lse[own]]
        top = levels[0]
        for level in levels[1:]:
            top = jnp.maximum(top, level)
        shares = [jnp.exp2(level - top) for level in levels]
        whole = shares[0]
        for share in shares[1:]:
            whole = whole + share
        shares = [share / whole for share in shares]
        for h in range(cols // HEAD_DIM):
            at = slice(h * HEAD_DIM, (h + 1) * HEAD_DIM)
            mixed = oown[:, at] * shares[own][:, h:h + 1]
            for slot in range(n - 1):
                mixed = mixed + orecv[slot, :, at].astype(jnp.float32) * shares[slot][:, h:h + 1]
            out_ref[:, at] = mixed.astype(jnp.bfloat16)
        for slot in range(n - 1):
            for c in range(chunks):
                q_copy(slot, c).wait_send()
                o_copy(slot, c).wait_send()
            l_copy(slot).wait_send()

    return kernel, chunks, groups


def solution(mesh):
    n = mesh.shape["ctx"]

    def local(query, slab_keys, slab_values, ctx_keys, ctx_values, prompt_len, cont_len, slab_order):
        rows, cols = query.shape
        keys = ctx_keys.shape[0]
        kernel, chunks, groups = make_kernel(n, rows, cols, keys, slab_order.shape[0])
        slab_pad = -(-rows // 128) * 128
        anywhere = pl.BlockSpec(memory_space=pl.ANY)
        bf16, f32 = jnp.bfloat16, jnp.float32
        dma = pltpu.SemaphoreType.DMA
        return pl.pallas_call(
            kernel,
            out_shape=pltpu.VMEM((rows, cols), bf16),
            in_specs=[anywhere] * 8,
            out_specs=pl.BlockSpec(memory_space=pltpu.VMEM),
            scratch_shapes=[
                pltpu.SMEM(prompt_len.shape, jnp.int32),
                pltpu.SMEM(cont_len.shape, jnp.int32),
                pltpu.SMEM(slab_order.shape, jnp.int32),
                pltpu.VMEM((n, rows, cols), bf16),
                pltpu.VMEM((groups, keys, HEAD_DIM), bf16),
                pltpu.VMEM((groups, keys, HEAD_DIM), bf16),
                pltpu.VMEM((groups, slab_pad, HEAD_DIM), bf16),
                pltpu.VMEM((groups, slab_pad, HEAD_DIM), bf16),
                pltpu.VMEM((n - 1, rows, cols), bf16),
                pltpu.VMEM((n - 1, rows, cols), bf16),
                pltpu.VMEM((rows, cols), f32),
                pltpu.VMEM((n, rows, 128), f32),
                pltpu.VMEM((n - 1, rows, 128), f32),
                dma((4 * groups + 4,)),
                dma((n - 1, chunks)),
                dma((n - 1, chunks)),
                dma((n - 1, chunks)),
                dma((n - 1, chunks)),
                dma((n - 1,)),
                dma((n - 1,)),
            ],
            compiler_params=pltpu.CompilerParams(
                collective_id=0, has_side_effects=True, vmem_limit_bytes=56 * 1024 * 1024),
        )(prompt_len, cont_len, slab_order, query, slab_keys, slab_values, ctx_keys, ctx_values)

    placed = (P(("rep", "ctx"), "kvh"),) * 5 + (P("rep"),) * 3
    return jax.shard_map(
        local, mesh=mesh, in_specs=placed, out_specs=P(("rep", "ctx"), "kvh"), check_vma=False)
```

```python
import jax
import jax.numpy as jnp
from jax import lax
from jax.experimental import pallas as pl
from jax.experimental.pallas import tpu as pltpu
from jax.sharding import PartitionSpec as P

HEADS = 128
KV_HEADS = 8
HEAD_DIM = 128
GROUP = HEADS // KV_HEADS
LOG2E = 1.4426950408889634
SCALE2 = HEAD_DIM ** -0.5 * LOG2E
LOWEST = -1e30
MESH = pl.DeviceIdType.MESH

CHUNK_HEADS = 8
LEAD = 2


def make_kernel(n, rows, cols, keys, spans):
    groups = cols // (GROUP * HEAD_DIM)
    width = CHUNK_HEADS * HEAD_DIM
    chunks = cols // width
    per_group = chunks // groups
    span = rows * n // spans
    local_spans = rows // span
    total_items = n * chunks
    own = n - 1
    heads = cols // HEAD_DIM
    side = 128 // heads
    blocks = rows // 8
    lead = LEAD

    def kernel(prompt_hbm, cont_hbm, order_hbm, q_hbm, sk_hbm, sv_hbm, ck_hbm, cv_hbm, out_ref,
               prompt_ref, cont_ref, order_ref, qbuf, kbuf, vbuf, skbuf, svbuf, osend, orecv, oown, lse, lrecv,
               local_sem, q_send, q_recv, o_send, o_recv, l_send, l_recv):
        me = lax.axis_index("ctx")

        barrier = pltpu.get_barrier_semaphore()
        for d in range(1, n):
            pl.semaphore_signal(barrier, inc=1, device_id={"ctx": lax.rem(me + d, n)}, device_id_type=MESH)

        local_copies = []
        for g in range(groups):
            lanes = slice(g * HEAD_DIM, (g + 1) * HEAD_DIM)
            for i, (src, dst) in enumerate((
                (ck_hbm.at[:, lanes], kbuf.at[g]),
                (cv_hbm.at[:, lanes], vbuf.at[g]),
                (sk_hbm.at[:, lanes], skbuf.at[g, 0:rows]),
                (sv_hbm.at[:, lanes], svbuf.at[g, 0:rows]),
            )):
                local_copies.append(pltpu.make_async_copy(src, dst, local_sem.at[g * 4 + i]))
        local_copies.append(pltpu.make_async_copy(q_hbm, qbuf.at[own], local_sem.at[groups * 4]))
        for i, (src, dst) in enumerate((
            (prompt_hbm, prompt_ref), (cont_hbm, cont_ref), (order_hbm, order_ref))):
            local_copies.append(pltpu.make_async_copy(src, dst, local_sem.at[groups * 4 + 1 + i]))
        for copy in local_copies:
            copy.start()

        pad = skbuf.shape[1] - rows
        for g in range(groups):
            skbuf[g, rows:, :] = jnp.zeros((pad, HEAD_DIM), jnp.bfloat16)
            svbuf[g, rows:, :] = jnp.zeros((pad, HEAD_DIM), jnp.bfloat16)

        pl.semaphore_wait(barrier, n - 1)

        def q_copy(slot, c):
            at = pl.ds(pl.multiple_of(c * width, width), width)
            return pltpu.make_async_remote_copy(
                src_ref=q_hbm.at[:, at], dst_ref=qbuf.at[slot, :, at],
                send_sem=q_send.at[slot, c], recv_sem=q_recv.at[slot, c],
                device_id={"ctx": lax.rem(me + slot + 1, n)}, device_id_type=MESH)

        def o_copy(slot, c):
            at = pl.ds(pl.multiple_of(c * width, width), width)
            return pltpu.make_async_remote_copy(
                src_ref=osend.at[slot, :, at], dst_ref=orecv.at[slot, :, at],
                send_sem=o_send.at[slot, c], recv_sem=o_recv.at[slot, c],
                device_id={"ctx": lax.rem(me + 2 * n - slot - 1, n)}, device_id_type=MESH)

        def l_copy(slot):
            return pltpu.make_async_remote_copy(
                src_ref=lse.at[slot], dst_ref=lrecv.at[slot],
                send_sem=l_send.at[slot], recv_sem=l_recv.at[slot],
                device_id={"ctx": lax.rem(me + 2 * n - slot - 1, n)}, device_id_type=MESH)

        for slot in range(n - 1):
            for c in range(chunks):
                q_copy(slot, c).start()
        for copy in local_copies:
            copy.wait()

        ends, prompts, at_end = [], [], 0
        for r in range(prompt_ref.shape[0]):
            at_end = at_end + cont_ref[r]
            ends.append(at_end)
            prompts.append(prompt_ref[r])

        def facts(shape, dim, device):
            ids = lax.broadcasted_iota(jnp.int32, shape, dim)
            place = ids
            for k in range(local_spans):
                start = order_ref[device * local_spans + k] * span - k * span
                inside = (ids >= k * span) & (ids < (k + 1) * span)
                place = jnp.where(inside, ids + start, place)
            roll = jnp.zeros(shape, jnp.int32)
            for end in ends:
                roll = roll + (place >= end).astype(jnp.int32)
            return place, roll

        key_place, key_roll = facts((rows, skbuf.shape[1]), 1, me)
        key_is = lax.broadcasted_iota(jnp.int32, (rows, skbuf.shape[1]), 1) < rows
        lane = lax.broadcasted_iota(jnp.int32, (8, 128), 1)

        def step(t, carry):
            item = lax.rem(t + total_items - lead, total_items)
            slot = item // chunks
            c = lax.rem(item, chunks)
            g = c // per_group
            source = lax.rem(me + 2 * n - slot - 1, n)

            @pl.when(slot < own)
            def _():
                q_copy(slot, c).wait_recv()

            row_place, row_roll = facts((rows, 128), 0, source)
            limit = jnp.zeros((rows, 128), jnp.int32)
            for r, prompt in enumerate(prompts):
                limit = jnp.where(row_roll == r, prompt, limit)
            limit = limit[:, :1] - me * keys
            slab_bias = jnp.where(
                key_is & (key_roll == row_roll) & (key_place <= row_place), 0.0, LOWEST)

            at = pl.ds(pl.multiple_of(c * width, width), width)
            q = qbuf[slot, :, at]
            q = jnp.concatenate(
                [q[:, h * HEAD_DIM:(h + 1) * HEAD_DIM] for h in range(CHUNK_HEADS)], axis=0)
            dims = (((1,), (1,)), ((), ()))
            s_ctx = lax.dot_general(q, kbuf[g], dims, preferred_element_type=jnp.float32)
            s_slab = lax.dot_general(q, skbuf[g], dims, preferred_element_type=jnp.float32)
            limits = jnp.concatenate([limit] * CHUNK_HEADS, axis=0)
            columns = lax.broadcasted_iota(jnp.int32, s_ctx.shape, 1)
            s_ctx = jnp.where(columns < limits, s_ctx, LOWEST)
            s_slab = s_slab + jnp.concatenate([slab_bias] * CHUNK_HEADS, axis=0)
            top = jnp.maximum(
                jnp.max(s_ctx, axis=1, keepdims=True), jnp.max(s_slab, axis=1, keepdims=True))
            p_ctx = jnp.exp2((s_ctx - top) * SCALE2)
            p_slab = jnp.exp2((s_slab - top) * SCALE2)
            total = jnp.sum(p_ctx, axis=1, keepdims=True) + jnp.sum(p_slab, axis=1, keepdims=True)
            o = jnp.dot(p_ctx.astype(jnp.bfloat16), vbuf[g], preferred_element_type=jnp.float32)
            o = o + jnp.dot(p_slab.astype(jnp.bfloat16), svbuf[g], preferred_element_type=jnp.float32)
            o = o * (1.0 / total)
            level = top * SCALE2 + jnp.log2(total)
            for band in range(lse.shape[1] // 8):
                levels = lse[slot, band * 8:band * 8 + 8]
                for h in range(CHUNK_HEADS):
                    for k in range(side):
                        first = h * rows + (band * side + k) * 8
                        levels = jnp.where(
                            lane == k * heads + c * CHUNK_HEADS + h, level[first:first + 8], levels)
                lse[slot, band * 8:band * 8 + 8] = levels
            o = jnp.concatenate(
                [o[h * rows:(h + 1) * rows] for h in range(CHUNK_HEADS)], axis=1)

            @pl.when(slot == own)
            def _():
                oown[:, at] = o

            @pl.when(slot < own)
            def _():
                osend[slot, :, at] = o.astype(jnp.bfloat16)

                @pl.when(c == chunks - 1)
                def _():
                    l_copy(slot).start()

                o_copy(slot, c).start()

            return carry

        for slot in range(n):
            lse[slot] = jnp.zeros(lse.shape[1:], jnp.float32)
        lax.fori_loop(0, total_items, step, 0)

        for slot in range(n - 1):
            l_copy(slot).wait_recv()
        levels = [lrecv[slot] for slot in range(n - 1)] + [lse[own]]
        top = levels[0]
        for level in levels[1:]:
            top = jnp.maximum(top, level)
        shares = [jnp.exp2(level - top) for level in levels]
        whole = shares[0]
        for share in shares[1:]:
            whole = whole + share
        shares = [share / whole for share in shares]

        def share_of(slot, h):
            return jnp.concatenate([
                shares[slot][k // side * 8:k // side * 8 + 8, k % side * heads + h:k % side * heads + h + 1]
                for k in range(blocks)], axis=0)

        for h in range(heads):
            if h % CHUNK_HEADS == 0:
                for slot in range(n - 1):
                    o_copy(slot, h // CHUNK_HEADS).wait_recv()
            at = slice(h * HEAD_DIM, (h + 1) * HEAD_DIM)
            mixed = oown[:, at] * share_of(own, h)
            for slot in range(n - 1):
                mixed = mixed + orecv[slot, :, at].astype(jnp.float32) * share_of(slot, h)
            out_ref[:, at] = mixed.astype(jnp.bfloat16)
        for slot in range(n - 1):
            for c in range(chunks):
                q_copy(slot, c).wait_send()
                o_copy(slot, c).wait_send()
            l_copy(slot).wait_send()

    return kernel, chunks, groups


def solution(mesh):
    n = mesh.shape["ctx"]

    def local(query, slab_keys, slab_values, ctx_keys, ctx_values, prompt_len, cont_len, slab_order):
        rows, cols = query.shape
        keys = ctx_keys.shape[0]
        kernel, chunks, groups = make_kernel(n, rows, cols, keys, slab_order.shape[0])
        level_rows = rows * (cols // HEAD_DIM) // 128
        slab_pad = -(-rows // 128) * 128
        anywhere = pl.BlockSpec(memory_space=pl.ANY)
        bf16, f32 = jnp.bfloat16, jnp.float32
        dma = pltpu.SemaphoreType.DMA
        return pl.pallas_call(
            kernel,
            out_shape=pltpu.VMEM((rows, cols), bf16),
            in_specs=[anywhere] * 8,
            out_specs=pl.BlockSpec(memory_space=pltpu.VMEM),
            scratch_shapes=[
                pltpu.SMEM(prompt_len.shape, jnp.int32),
                pltpu.SMEM(cont_len.shape, jnp.int32),
                pltpu.SMEM(slab_order.shape, jnp.int32),
                pltpu.VMEM((n, rows, cols), bf16),
                pltpu.VMEM((groups, keys, HEAD_DIM), bf16),
                pltpu.VMEM((groups, keys, HEAD_DIM), bf16),
                pltpu.VMEM((groups, slab_pad, HEAD_DIM), bf16),
                pltpu.VMEM((groups, slab_pad, HEAD_DIM), bf16),
                pltpu.VMEM((n - 1, rows, cols), bf16),
                pltpu.VMEM((n - 1, rows, cols), bf16),
                pltpu.VMEM((rows, cols), f32),
                pltpu.VMEM((n, level_rows, 128), f32),
                pltpu.VMEM((n - 1, level_rows, 128), f32),
                dma((4 * groups + 4,)),
                dma((n - 1, chunks)),
                dma((n - 1, chunks)),
                dma((n - 1, chunks)),
                dma((n - 1, chunks)),
                dma((n - 1,)),
                dma((n - 1,)),
            ],
            compiler_params=pltpu.CompilerParams(
                collective_id=0, has_side_effects=True, vmem_limit_bytes=56 * 1024 * 1024),
        )(prompt_len, cont_len, slab_order, query, slab_keys, slab_values, ctx_keys, ctx_values)

    placed = (P(("rep", "ctx"), "kvh"),) * 5 + (P("rep"),) * 3
    return jax.shard_map(
        local, mesh=mesh, in_specs=placed, out_specs=P(("rep", "ctx"), "kvh"), check_vma=False)
```
